32 devices in a mesh: rows: 8 (over y, x, core), cols: 4 (over z).
Axes of the slice: x: 2, y: 2, z: 4, core: 2. Of those that a mesh axis runs over, the one named last changes fastest.
Arguments:
- blocks: float32 [32, 4, 16, 128, 128], P('rows', 'cols'), may hold values from -0.125 to 0.125
- ell_index: int32 [32, 4, 16], P('rows', 'cols'), may hold values from 0 to 31, as said below
- counts: int32 [32, 4], P('rows', 'cols'), may hold values from 4 to 16, as said below
- objective: float32 [16384], P('cols'), may hold values from -6 to 6
- lower_bound: float32 [16384], P('cols'), may hold values from -0.4 to -0.05
- upper_bound: float32 [16384], P('cols'), may hold values from 0.05 to 0.4
- var_kind: int32 [16384], P('cols'), may hold values from 0 to 2
- demand: float32 [32, 4096], P(None, 'rows'), may hold values from -6 to 6
- row_kind: int32 [4096], P('rows'), may hold values from 0 to 1
- step_size: float32 [32], replicated, may hold values from 0.2 to 0.5
- primal_weight: float32 [32], replicated, may hold values from 0.5 to 2
Outputs:
- primal: float32 [32, 16384], P(None, 'cols')
- dual_vector: float32 [32, 4096], P(None, 'rows')
- final_weight: float32 [32], replicated
The draws below stay inside these ranges and needn't reach their ends.
Inputs may be any that keep to these rules, and one draw needn't show every extreme that they name: Slots in use: for each row block r and column group c, slots 0 to counts[r, c] - 1 are in use; slots from counts[r, c] on to 15 are padding, and their blocks and ell_index entries are ignored. `ell_index`: the slots of one row block in one column group name distinct column blocks of that group.
All inputs are finite; a program needn't handle non-finite values.
Results may differ from the reference program's by a relative error of at most 0.0002.
Values sent between devices are 32-bit elements; how exact they have to be, the bound alone decides.
A program may use at most 64 MiB of HBM per device.

```python
import math
import jax
import jax.numpy as jnp
from jax import lax

BS = 128
W = 16
S = 32
ITERS = 4
CB = 32
NRB = 32
M = 4096
NV = 16384
N_COLS = 4


def draw_counts(key, part):
    key = jax.random.fold_in(key, 11)
    first, second, third = jax.random.split(key, 3)
    shape = (NRB, N_COLS)
    dense = jax.random.randint(first, shape, 0, 4) == 0
    sparse_count = jax.random.randint(second, shape, 4, W // 2 + 1)
    dense_count = jax.random.randint(third, shape, W // 2 + 1, W + 1)
    result = jnp.where(dense, dense_count, sparse_count)
    return result.at[0, 0].set(W).astype(jnp.int32)


def draw_ell_index(key, part):
    key = jax.random.fold_in(key, 23)
    scores = jax.random.randint(key, (NRB, N_COLS, CB), 0, 1 << 20) * CB + jnp.arange(CB, dtype=jnp.int32)
    order = jnp.argsort(scores, axis=-1)
    return order[..., :W].astype(jnp.int32)


def plant(drawn, stream_key, smallest, high):
    longest = drawn.shape.index(max(drawn.shape))
    spots = []
    for shift in (0, 1):
        where = [jax.random.randint(jax.random.fold_in(stream_key, axis), (), 0, length) for axis, length in enumerate(drawn.shape)]
        where[longest] = (where[longest] + shift) % drawn.shape[longest]
        spots.append(tuple(where))
    return drawn.at[spots[0]].set(smallest).at[spots[1]].set(high)


def block_scale(own_key, extent, shards, low, top_value):
    def one(position, parts):
        heights = jax.random.uniform(jax.random.fold_in(jax.random.fold_in(own_key, 6), position), (parts,), jnp.float32, low / len(shards), top_value / len(shards))
        return jnp.repeat(jnp.exp(heights), extent[position] // parts).reshape((-1,) + (1,) * (len(extent) - position - 1))

    gain = one(*shards[0])
    for cut in shards[1:]:
        gain = gain * one(*cut)
    return gain


def scatter_about(key, shape, spread, bound, cuts=(), kind=jnp.bfloat16):
    array = jax.random.normal(key, shape, jnp.float32) * spread
    if len(cuts) > 0:
        array = block_scale(key, shape, cuts, -0.22, 0.18) * array
    return jnp.clip(array, min=-bound, max=bound).astype(kind)


def setup_inputs(seed: int = 0) -> dict:
    keys = jax.random.split(jax.random.key(seed), 12)
    return {
        "blocks": scatter_about(keys[0], (NRB, N_COLS, W, BS, BS), (4 * BS * N_COLS) ** -0.5, 0.125, ((0, 8), (1, 4)), jnp.float32),
        "ell_index": draw_ell_index(jax.random.fold_in(keys[11], 71), 0),
        "counts": draw_counts(jax.random.fold_in(keys[11], 71), 0),
        "objective": scatter_about(keys[3], (NV,), 1.0, 6.0, ((0, 4),), jnp.float32),
        "lower_bound": jnp.clip(-0.4 + 0.35 * jax.random.uniform(keys[4], (NV,), jnp.float32) ** block_scale(keys[4], (NV,), ((0, 4),), -0.2, 0.2), -0.4, -0.05),
        "upper_bound": jnp.clip(0.05 + 0.35 * jax.random.uniform(keys[5], (NV,), jnp.float32) ** block_scale(keys[5], (NV,), ((0, 4),), -0.2, 0.2), 0.05, 0.4),
        "var_kind": plant(jax.random.randint(keys[6], (NV,), 0, 3), jax.random.fold_in(keys[6], 1), 0, 2).astype(jnp.int32),
        "demand": scatter_about(keys[7], (S, M), 1.0, 6.0, ((1, 8),), jnp.float32),
        "row_kind": plant(jax.random.randint(keys[8], (M,), 0, 2), jax.random.fold_in(keys[8], 1), 0, 1).astype(jnp.int32),
        "step_size": jnp.clip(jnp.exp(jax.random.uniform(keys[9], (S,), jnp.float32, math.log(0.2), math.log(0.5))), 0.2, 0.5),
        "primal_weight": jnp.clip(jnp.exp(jax.random.uniform(keys[10], (S,), jnp.float32, math.log(0.5), math.log(2.0))), 0.5, 2.0),
    }


epsilon = 1e-06
highest = lax.Precision.HIGHEST

def project_primal(values, var_kind, lower_bound, upper_bound):
    floored = jnp.maximum(values, lower_bound[None, :])
    boxed = jnp.minimum(floored, upper_bound[None, :])
    kinds = var_kind[None, :]
    return jnp.where(kinds == 0, values, jnp.where(kinds == 1, floored, boxed))

def project_dual(values, row_kind):
    return jnp.where(row_kind[None, :] == 1, jnp.maximum(values, 0.0), values)

def apply_forward(blocks, column_ids, live_mask, field):
    scenarios = field.shape[0]
    field_blocks = field.reshape(scenarios, -1, BS)

    def one_row(pieces):
        tiles, ids, live = pieces
        taken = field_blocks[:, ids] * live[None, :, :, None]
        return jnp.einsum('cwij,scwj->si', tiles, taken, precision=highest)
    result = lax.map(one_row, (blocks, column_ids, live_mask))
    return jnp.transpose(result, (1, 0, 2)).reshape(scenarios, -1)

def apply_backward(blocks, column_ids, live_mask, dual_values):
    scenarios = dual_values.shape[0]
    row_values = jnp.transpose(dual_values.reshape(scenarios, -1, BS), (1, 0, 2))

    def one_row(carry, pieces):
        tiles, ids, live, values = pieces
        terms = jnp.einsum('cwij,si->scwj', tiles, values, precision=highest) * live[None, :, :, None]
        return (carry.at[:, ids].add(terms), None)
    start = jnp.zeros((scenarios, NV // BS, BS), jnp.float32)
    result, unused = lax.scan(one_row, start, (blocks, column_ids, live_mask, row_values))
    return result.reshape(scenarios, -1)

def reference(blocks, ell_index, counts, objective, lower_bound, upper_bound, var_kind, demand, row_kind, step_size, primal_weight):
    offsets = (jnp.arange(N_COLS, dtype=jnp.int32) * CB).astype(jnp.int32)
    column_ids = (ell_index + offsets[None, :, None]).astype(jnp.int32)
    live_mask = (jnp.arange(W, dtype=jnp.int32)[None, None, :] < counts[:, :, None]).astype(jnp.float32)
    primal = jnp.zeros((S, NV), jnp.float32)
    dual_vector = jnp.zeros((S, M), jnp.float32)
    weight = primal_weight
    for iteration in range(ITERS):
        dual_image = apply_backward(blocks, column_ids, live_mask, dual_vector)
        primal_step = (step_size / weight)[:, None]
        dual_step = (step_size * weight)[:, None]
        new_primal = project_primal(primal - primal_step * (objective[None, :] - dual_image), var_kind, lower_bound, upper_bound)
        primal_image = apply_forward(blocks, column_ids, live_mask, 2.0 * new_primal - primal)
        new_dual = project_dual(dual_vector + dual_step * (demand - primal_image), row_kind)
        primal_move = lax.optimization_barrier(jnp.sum((new_primal - primal) ** 2, axis=1))
        dual_move = lax.optimization_barrier(jnp.sum((new_dual - dual_vector) ** 2, axis=1))
        weight = jnp.sqrt(weight * jnp.sqrt((dual_move + epsilon) / (primal_move + epsilon)))
        primal = new_primal
        dual_vector = new_dual
    return (primal, dual_vector, weight)
```

```python
import functools

import jax
import jax.numpy as jnp
from jax import lax
from jax.experimental import pallas as pl
from jax.experimental.pallas import tpu as pltpu
from jax.sharding import PartitionSpec as P

ITERS = 4
EPS = 1e-06
LANES = 128
MESH = pl.DeviceIdType.MESH
f32 = jnp.float32
bf16 = jnp.bfloat16


def split(values):
    high = values.astype(bf16)
    low = (values - high.astype(f32)).astype(bf16)
    return high, low


def matmul(left, right, transposed):
    dims = (((1,), (1 if transposed else 0,)), ((), ()))
    return lax.dot_general(left, right, dims, preferred_element_type=f32)


def kernel(
    R,
    C,
    slot_ref,
    blocks_ref,
    obj_ref,
    lb_ref,
    ub_ref,
    vk_ref,
    demand_ref,
    rk_ref,
    step_ref,
    pw_ref,
    x_ref,
    u_ref,
    w_ref,
    k_hi,
    k_lo,
    a_src,
    a_dst,
    b_src,
    b_dst,
    x_new,
    x_old,
    d_src,
    d_dst,
    e_buf,
    n_buf,
    steps,
    weights,
    a_sem,
    b_sem,
    c_sem,
    f_sem,
    d_sem,
    e_sem,
    n_sem,
):
    me = lax.axis_index("rows")
    col = lax.axis_index("cols")
    core = lax.rem(me, 2)
    chip = lax.div(me, 2)
    sibling = me + 1 - 2 * core
    chips = R // 2
    row_blocks, width = blocks_ref.shape[0], blocks_ref.shape[2]
    rows = row_blocks * width
    S = x_ref.shape[0]
    part = S // C
    chunk = x_new.shape[2]
    tiles = chunk // width
    group = LANES // C

    barrier = pltpu.get_barrier_semaphore()
    for o in range(1, R):
        pl.semaphore_signal(barrier, inc=1, device_id={"rows": lax.rem(me + o, R)}, device_id_type=MESH)
    for o in range(1, C):
        pl.semaphore_signal(barrier, inc=1, device_id={"cols": lax.rem(col + o, C)}, device_id_type=MESH)

    def copy(src, dst, sem, o, axis, target):
        return pltpu.make_async_remote_copy(
            src_ref=src,
            dst_ref=dst,
            send_sem=sem.at[0, o],
            recv_sem=sem.at[1, o],
            device_id={axis: target},
            device_id_type=MESH,
        )

    def chip_at(o):
        return lax.rem(chip + o, chips)

    def chip_from(o):
        return lax.rem(chip + chips - o, chips)

    eye = lax.broadcasted_iota(jnp.int32, (S, S), 0) == lax.broadcasted_iota(jnp.int32, (S, S), 1)

    def upright(ref):
        return jnp.sum(jnp.where(eye, jnp.broadcast_to(ref[...], (S, S)), 0.0), axis=1, keepdims=True)

    step_all = upright(step_ref)
    weight_all = upright(pw_ref)
    for k in range(C):
        rows_k = slice(k * part, (k + 1) * part)
        steps[k] = jnp.broadcast_to(step_all[rows_k], (part, LANES))
        weights[k] = jnp.broadcast_to(weight_all[rows_k], (part, LANES))

    def stacked(ref):
        return jnp.concatenate([ref[k] for k in range(C)], axis=0)

    def project(values, at):
        lb, ub, kind = lb_ref[:, at], ub_ref[:, at], vk_ref[:, at]
        floored = jnp.maximum(values, lb)
        boxed = jnp.minimum(floored, ub)
        return jnp.where(kind == 0, values, jnp.where(kind == 1, floored, boxed))

    def columns(q):
        return pl.ds(pl.multiple_of(q * chunk, LANES), chunk)

    def forward(field, q):
        high, low = split(field)
        both = matmul(jnp.concatenate([high, low], axis=0), k_hi[q], True)
        return both[:S] + both[S:] + matmul(high, k_lo[q], True)

    def cols_phase(total, primal_part, old_dual):
        moved = jnp.broadcast_to(primal_part, (S, LANES))
        for k in range(C):
            rows_k = slice(k * part, (k + 1) * part)
            d_src[k, :, :rows] = total[rows_k]
            d_src[k, :, rows:] = moved[rows_k]
        sends = []
        for o in range(1, C):
            target = lax.rem(col + o, C)
            c = copy(d_src.at[target], d_dst.at[col], d_sem, o, "cols", target)
            c.start()
            sends.append(c)
        image = d_src[col]
        for o in range(1, C):
            source = lax.rem(col + C - o, C)
            copy(d_src.at[source], d_dst.at[source], d_sem, o, "cols", source).wait_recv()
            image = image + d_dst[source]
        sigma = (steps[col] * weights[col])[:, :1]
        fresh = old_dual + sigma * (demand_ref[col] - image[:, :rows])
        fresh = jnp.where(rk_ref[...] == 1, jnp.maximum(fresh, 0.0), fresh)
        dual_part = jnp.sum((fresh - old_dual) ** 2, axis=1, keepdims=True)
        lane = lax.broadcasted_iota(jnp.int32, (part, LANES), 1)
        e_buf[col, :, :rows] = fresh
        e_buf[col, :, rows:] = jnp.where(lane < LANES // 2, image[:, rows:], dual_part)
        for o in range(1, C):
            target = lax.rem(col + o, C)
            c = copy(e_buf.at[col], e_buf.at[col], e_sem, o, "cols", target)
            c.start()
            sends.append(c)
        for o in range(1, C):
            source = lax.rem(col + C - o, C)
            copy(e_buf.at[source], e_buf.at[source], e_sem, o, "cols", source).wait_recv()
        norms = jnp.zeros((part, LANES), f32)
        for k in range(C):
            moves = e_buf[k, :, rows:]
            pair = jnp.where(lax.rem(lane, group) < group // 2, moves[:, :1], moves[:, LANES // 2 : LANES // 2 + 1])
            norms = jnp.where(lax.div(lane, group) == k, pair, norms)
        n_buf[me] = norms
        for o in range(1, R):
            copy(n_buf.at[me], n_buf.at[me], n_sem, o, "rows", lax.rem(me + o, R)).start()
        for c in sends:
            c.wait_send()

    def take_norms():
        for o in range(1, R):
            source = lax.rem(me + R - o, R)
            copy(n_buf.at[source], n_buf.at[source], n_sem, o, "rows", source).wait_recv()
        norms = n_buf[0]
        for r in range(1, R):
            norms = norms + n_buf[r]
        for k in range(C):
            primal_move = norms[:, k * group : k * group + 1]
            dual_move = norms[:, k * group + group // 2 : k * group + group // 2 + 1]
            ratio = (dual_move + EPS) / (primal_move + EPS)
            weights[k] = jnp.sqrt(weights[k] * jnp.sqrt(ratio))
        for o in range(1, R):
            copy(n_buf.at[me], n_buf.at[me], n_sem, o, "rows", lax.rem(me + o, R)).wait_send()

    tau = (stacked(steps) / stacked(weights))[:, :1]

    def first(q, total):
        for r in range(row_blocks):
            for t in range(tiles):
                slot = slot_ref[r, q * tiles + t]
                tile = blocks_ref[r, jnp.maximum(slot, 0)]
                tile = jnp.where(slot >= 0, tile, 0.0)
                high, low = split(tile)
                k_hi[q, r * width : (r + 1) * width, t * width : (t + 1) * width] = high
                k_lo[q, r * width : (r + 1) * width, t * width : (t + 1) * width] = low
        at = columns(q)
        fresh = project(-tau * obj_ref[:, at], at)
        x_old[q] = fresh
        return total + forward(2.0 * fresh, q)

    total = lax.fori_loop(0, R, first, jnp.zeros((S, rows), f32))
    pl.semaphore_wait(barrier, R + C - 2)
    own = x_old[me]
    cols_phase(total, jnp.sum(own * own, axis=1, keepdims=True), jnp.zeros((part, rows), f32))

    def iteration(step, carry):
        dual = jnp.concatenate([e_buf[k, :, :rows] for k in range(C)], axis=0)
        dual_hi, dual_lo = split(dual)
        dual_both = jnp.concatenate([dual_hi, dual_lo], axis=0)

        def backward(q):
            both = matmul(dual_both, k_hi[q], False)
            return both[:S] + both[S:] + matmul(dual_hi, k_lo[q], False)

        sends = []
        order = list(range(1, chips)) + [0]
        for o in order:
            p = chip_at(o)
            a_src[o] = backward(2 * p + 1 - core)
            c = copy(a_src.at[o], a_dst.at[p], a_sem, o, "rows", sibling)
            c.start()
            sends.append(c)
        for o in order:
            p = chip_at(o)
            mine = backward(2 * p + core)
            copy(a_src.at[o], a_dst.at[p], a_sem, o, "rows", sibling).wait_recv()
            mine = mine + a_dst[p]
            if o > 0:
                b_src[o] = mine
                c = copy(b_src.at[o], b_dst.at[o], b_sem, o, "rows", 2 * p + core)
                c.start()
                sends.append(c)
        take_norms()
        tau = (stacked(steps) / stacked(weights))[:, :1]
        image = mine
        for o in range(1, chips):
            copy(b_src.at[o], b_dst.at[o], b_sem, o, "rows", 2 * chip_at(o) + core).wait_recv()
            image = image + b_dst[o]
        at = columns(me)
        before = x_old[me]
        fresh = project(before - tau * (obj_ref[:, at] - image), at)
        x_new[me] = fresh
        for o in range(1, chips):
            c = copy(x_new.at[me], x_new.at[me], c_sem, o, "rows", 2 * chip_at(o) + core)
            c.start()
            sends.append(c)
        c = copy(x_new.at[me], x_new.at[me], c_sem, 0, "rows", sibling)
        c.start()
        sends.append(c)
        primal_part = jnp.sum((fresh - before) ** 2, axis=1, keepdims=True)
        x_old[me] = fresh
        total = forward(2.0 * fresh - before, me)

        def add(q, total):
            now = x_new[q]
            field = 2.0 * now - x_old[q]
            x_old[q] = now
            return total + forward(field, q)

        copy(x_new.at[sibling], x_new.at[sibling], c_sem, 0, "rows", sibling).wait_recv()
        total = add(sibling, total)
        for o in range(1, chips):
            q = 2 * chip_from(o) + core
            copy(x_new.at[q], x_new.at[q], c_sem, o, "rows", q).wait_recv()
            c = copy(x_new.at[q], x_new.at[q], f_sem, o, "rows", sibling)
            c.start()
            sends.append(c)
            total = add(q, total)
        for o in range(1, chips):
            q = 2 * chip_from(o) + 1 - core
            copy(x_new.at[q], x_new.at[q], f_sem, o, "rows", sibling).wait_recv()
            total = add(q, total)
        for c in sends:
            c.wait_send()
        cols_phase(total, primal_part, e_buf[col, :, :rows])
        return carry

    lax.fori_loop(1, ITERS, iteration, 0)
    take_norms()
    for q in range(R):
        x_ref[:, q * chunk : (q + 1) * chunk] = x_old[q]
    u_ref[...] = jnp.concatenate([e_buf[k, :, :rows] for k in range(C)], axis=0)
    final = jnp.broadcast_to(stacked(weights)[:, :1], (S, S))
    w_ref[...] = jnp.sum(jnp.where(eye, final, 0.0), axis=0, keepdims=True)


def solution(mesh):
    R, C = mesh.shape["rows"], mesh.shape["cols"]

    def local(blocks, ell_index, counts, objective, lower, upper, var_kind, demand, row_kind, step_size, primal_weight):
        row_blocks, _, slots, width, _ = blocks.shape
        n_vars = objective.shape[0]
        S, rows = demand.shape
        part, chunk = S // C, n_vars // R
        groups = n_vars // width
        ids = ell_index.reshape(row_blocks, slots)
        used = jnp.arange(slots, dtype=jnp.int32)[None, :] < counts.reshape(row_blocks, 1)
        hit = (ids[:, None, :] == jnp.arange(groups, dtype=jnp.int32)[None, :, None]) & used[:, None, :]
        slot_of = jnp.sum(jnp.where(hit, jnp.arange(1, slots + 1, dtype=jnp.int32)[None, None, :], 0), axis=2) - 1
        vmem = pl.BlockSpec(memory_space=pltpu.VMEM)
        primal, dual, weight = pl.pallas_call(
            functools.partial(kernel, R, C),
            out_shape=(
                jax.ShapeDtypeStruct((S, n_vars), f32),
                jax.ShapeDtypeStruct((S, rows), f32),
                jax.ShapeDtypeStruct((1, S), f32),
            ),
            in_specs=[pl.BlockSpec(memory_space=pltpu.SMEM)] + [vmem] * 9,
            out_specs=(vmem, vmem, vmem),
            scratch_shapes=[
                pltpu.VMEM((R, rows, chunk), bf16),
                pltpu.VMEM((R, rows, chunk), bf16),
                pltpu.VMEM((R // 2, S, chunk), f32),
                pltpu.VMEM((R // 2, S, chunk), f32),
                pltpu.VMEM((R // 2, S, chunk), f32),
                pltpu.VMEM((R // 2, S, chunk), f32),
                pltpu.VMEM((R, S, chunk), f32),
                pltpu.VMEM((R, S, chunk), f32),
                pltpu.VMEM((C, part, rows + LANES), f32),
                pltpu.VMEM((C, part, rows + LANES), f32),
                pltpu.VMEM((C, part, rows + LANES), f32),
                pltpu.VMEM((R, part, LANES), f32),
                pltpu.VMEM((C, part, LANES), f32),
                pltpu.VMEM((C, part, LANES), f32),
                pltpu.SemaphoreType.DMA((2, R // 2)),
                pltpu.SemaphoreType.DMA((2, R // 2)),
                pltpu.SemaphoreType.DMA((2, R // 2)),
                pltpu.SemaphoreType.DMA((2, R // 2)),
                pltpu.SemaphoreType.DMA((2, C)),
                pltpu.SemaphoreType.DMA((2, C)),
                pltpu.SemaphoreType.DMA((2, R)),
            ],
            compiler_params=pltpu.CompilerParams(
                collective_id=0, has_side_effects=True, vmem_limit_bytes=48 * 1024 * 1024
            ),
        )(
            slot_of,
            blocks.reshape(row_blocks, slots, width, width),
            objective.reshape(1, n_vars),
            lower.reshape(1, n_vars),
            upper.reshape(1, n_vars),
            var_kind.reshape(1, n_vars),
            demand.reshape(C, part, rows),
            row_kind.reshape(1, rows),
            step_size.reshape(1, S),
            primal_weight.reshape(1, S),
        )
        return primal, dual, weight.reshape(S)

    return jax.shard_map(
        local,
        mesh=mesh,
        in_specs=(
            P("rows", "cols", None, None, None),
            P("rows", "cols", None),
            P("rows", "cols"),
            P("cols"),
            P("cols"),
            P("cols"),
            P("cols"),
            P(None, "rows"),
            P("rows"),
            P(),
            P(),
        ),
        out_specs=(P(None, "cols"), P(None, "rows"), P()),
        check_vma=False,
    )
```

```python
import functools

import jax
import jax.numpy as jnp
from jax import lax
from jax.experimental import pallas as pl
from jax.experimental.pallas import tpu as pltpu
from jax.sharding import PartitionSpec as P

ITERS = 4
HALVES = 2
SUB = 8
EPS = 1e-06
LANES = 128
MESH = pl.DeviceIdType.MESH
f32 = jnp.float32
bf16 = jnp.bfloat16


def split(values):
    high = values.astype(bf16)
    low = (values - high.astype(f32)).astype(bf16)
    return high, low


def matmul(left, right, transposed):
    dims = (((1,), (1 if transposed else 0,)), ((), ()))
    return lax.dot_general(left, right, dims, preferred_element_type=f32)


def kernel(
    R,
    C,
    blocks_hbm,
    ids_hbm,
    counts_hbm,
    obj_hbm,
    lb_hbm,
    ub_hbm,
    vk_hbm,
    demand_hbm,
    rk_hbm,
    step_hbm,
    pw_hbm,
    x_hbm,
    u_hbm,
    w_ref,
    blocks_ref,
    ids_ref,
    counts_ref,
    obj_ref,
    lb_ref,
    ub_ref,
    vk_ref,
    demand_ref,
    rk_ref,
    step_ref,
    pw_ref,
    slot_vmem,
    slot_ref,
    k_hi,
    k_lo,
    a_src,
    a_dst,
    b_src,
    b_dst,
    x_new,
    x_old,
    d_buf,
    u_buf,
    p_buf,
    n_buf,
    steps,
    weights,
    in_sem,
    out_sem,
    a_sem,
    b_sem,
    c_sem,
    f_sem,
    d_sem,
    p_sem,
    n_sem,
):
    me = lax.axis_index("rows")
    col = lax.axis_index("cols")
    core = lax.rem(me, 2)
    chip = lax.div(me, 2)
    sibling = me + 1 - 2 * core
    chips = R // 2
    row_blocks, slots, width = blocks_ref.shape[0], blocks_ref.shape[1], blocks_ref.shape[2]
    rows = row_blocks * width
    S = demand_ref.shape[0]
    H = HALVES
    n = S // H
    chunk = x_new.shape[3]
    tiles = chunk // width
    groups = S // SUB
    group = LANES // groups

    loads = []
    pairs = (
        (ids_hbm, ids_ref),
        (counts_hbm, counts_ref),
        (blocks_hbm.at[:, 0], blocks_ref),
        (step_hbm, step_ref),
        (pw_hbm, pw_ref),
        (obj_hbm, obj_ref),
        (lb_hbm, lb_ref),
        (ub_hbm, ub_ref),
        (vk_hbm, vk_ref),
        (demand_hbm, demand_ref),
        (rk_hbm, rk_ref),
    )
    for i, (src, dst) in enumerate(pairs):
        c = pltpu.make_async_copy(src, dst, in_sem.at[i])
        c.start()
        loads.append(c)

    barrier = pltpu.get_barrier_semaphore()
    for o in range(1, R):
        pl.semaphore_signal(barrier, inc=1, device_id={"rows": lax.rem(me + o, R)}, device_id_type=MESH)
    for o in range(1, C):
        pl.semaphore_signal(barrier, inc=1, device_id={"cols": lax.rem(col + o, C)}, device_id_type=MESH)

    loads[0].wait()
    loads[1].wait()
    lane4 = lax.broadcasted_iota(jnp.int32, (row_blocks, LANES), 1)
    slot_of = jnp.full((row_blocks, LANES), -1, jnp.int32)
    square = (row_blocks, row_blocks)
    same = lax.broadcasted_iota(jnp.int32, square, 0) == lax.broadcasted_iota(jnp.int32, square, 1)
    counts = jnp.broadcast_to(counts_ref[...], square).astype(f32)
    counts = jnp.sum(jnp.where(same, counts, 0.0), axis=1, keepdims=True)
    ids = ids_ref[:, 0, :]
    for w in range(slots):
        slot_of = jnp.where((ids[:, w : w + 1] == lane4) & (counts > w + 0.5), w, slot_of)
    slot_vmem[...] = slot_of
    c = pltpu.make_async_copy(slot_vmem, slot_ref, in_sem.at[len(pairs)])
    c.start()
    for load in loads[2:]:
        load.wait()
    c.wait()

    def copy(src, dst, sem, at, axis, target):
        return pltpu.make_async_remote_copy(
            src_ref=src,
            dst_ref=dst,
            send_sem=sem.at[(0,) + at],
            recv_sem=sem.at[(1,) + at],
            device_id={axis: target},
            device_id_type=MESH,
        )

    def chip_at(o):
        return lax.rem(chip + o, chips)

    def chip_from(o):
        return lax.rem(chip + chips - o, chips)

    eye = lax.broadcasted_iota(jnp.int32, (S, S), 0) == lax.broadcasted_iota(jnp.int32, (S, S), 1)

    def upright(ref):
        return jnp.sum(jnp.where(eye, jnp.broadcast_to(ref[...], (S, S)), 0.0), axis=1, keepdims=True)

    steps[...] = jnp.broadcast_to(upright(step_ref), (S, LANES))
    weights[...] = jnp.broadcast_to(upright(pw_ref), (S, LANES))
    lane = lax.broadcasted_iota(jnp.int32, (SUB, LANES), 1)

    def pack(parts):
        column = jnp.concatenate(parts, axis=0)
        tile = jnp.zeros((SUB, LANES), f32)
        for k in range(groups):
            tile = jnp.where(lax.div(lane, group) == k, column[k * SUB : (k + 1) * SUB], tile)
        return tile

    def project(values, at):
        lb, ub, kind = lb_ref[:, at], ub_ref[:, at], vk_ref[:, at]
        floored = jnp.maximum(values, lb)
        boxed = jnp.minimum(floored, ub)
        return jnp.where(kind == 0, values, jnp.where(kind == 1, floored, boxed))

    def columns(q):
        return pl.ds(pl.multiple_of(q * chunk, LANES), chunk)

    def half(h):
        return slice(h * n, (h + 1) * n)

    def forward(field, q):
        high, low = split(field)
        m = field.shape[0]
        both = matmul(jnp.concatenate([high, low], axis=0), k_hi[q], True)
        return both[:m] + both[m:] + matmul(high, k_lo[q], True)

    def give_total(h, parity, total):
        d_buf[parity, h, col] = total
        for o in range(1, C):
            block = d_buf.at[parity, h, col]
            copy(block, block, d_sem, (parity, h, o), "cols", lax.rem(col + o, C)).start()

    def give_primal(parity, parts):
        p_buf[parity, col] = pack(parts)
        for o in range(1, C):
            block = p_buf.at[parity, col]
            copy(block, block, p_sem, (parity, o), "cols", lax.rem(col + o, C)).start()

    def dual_half(h, parity):
        for o in range(1, C):
            block = d_buf.at[parity, h, lax.rem(col + C - o, C)]
            copy(block, block, d_sem, (parity, h, o), "cols", lax.rem(col + o, C)).wait_recv()
        image = d_buf[parity, h, 0]
        for k in range(1, C):
            image = image + d_buf[parity, h, k]
        sigma = (steps[half(h)] * weights[half(h)])[:, :1]
        old = u_buf[h]
        fresh = old + sigma * (demand_ref[half(h)] - image)
        fresh = jnp.where(rk_ref[...] == 1, jnp.maximum(fresh, 0.0), fresh)
        u_buf[h] = fresh
        return fresh, jnp.sum((fresh - old) ** 2, axis=1, keepdims=True)

    def give_norms(parity, dual_parts):
        for o in range(1, C):
            block = p_buf.at[parity, lax.rem(col + C - o, C)]
            copy(block, block, p_sem, (parity, o), "cols", lax.rem(col + o, C)).wait_recv()
        moved = p_buf[parity, 0]
        for k in range(1, C):
            moved = moved + p_buf[parity, k]
        n_buf[me] = jnp.where(lax.rem(lane, group) < group // 2, moved, pack(dual_parts))
        for o in range(1, R):
            copy(n_buf.at[me], n_buf.at[me], n_sem, (o,), "rows", lax.rem(me + o, R)).start()
        for o in range(1, C):
            block = p_buf.at[parity, col]
            copy(block, block, p_sem, (parity, o), "cols", lax.rem(col + o, C)).wait_send()
            for h in range(H):
                block = d_buf.at[parity, h, col]
                copy(block, block, d_sem, (parity, h, o), "cols", lax.rem(col + o, C)).wait_send()

    def take_norms():
        for o in range(1, R):
            block = n_buf.at[lax.rem(me + R - o, R)]
            copy(block, block, n_sem, (o,), "rows", lax.rem(me + o, R)).wait_recv()
        norms = n_buf[0]
        for r in range(1, R):
            norms = norms + n_buf[r]
        primal_move = jnp.concatenate([norms[:, k * group : k * group + 1] for k in range(groups)], axis=0)
        middle = group // 2
        dual_move = jnp.concatenate([norms[:, k * group + middle : k * group + middle + 1] for k in range(groups)], axis=0)
        ratio = (dual_move + EPS) / (primal_move + EPS)
        weights[...] = jnp.sqrt(weights[...] * jnp.broadcast_to(jnp.sqrt(ratio), (S, LANES)))
        for o in range(1, R):
            copy(n_buf.at[me], n_buf.at[me], n_sem, (o,), "rows", lax.rem(me + o, R)).wait_send()

    first_tau = (steps[...] / weights[...])[:, :1]

    def first(q, total):
        for r in range(row_blocks):
            for t in range(tiles):
                slot = slot_ref[r, q * tiles + t]
                tile = blocks_ref[r, jnp.maximum(slot, 0)]
                tile = jnp.where(slot >= 0, tile, 0.0)
                high, low = split(tile)
                k_hi[q, r * width : (r + 1) * width, t * width : (t + 1) * width] = high
                k_lo[q, r * width : (r + 1) * width, t * width : (t + 1) * width] = low
        at = columns(q)
        fresh = project(-first_tau * obj_ref[:, at], at)
        for h in range(H):
            x_old[h, q] = fresh[half(h)]
        return total + forward(2.0 * fresh, q)

    total = lax.fori_loop(0, R, first, jnp.zeros((S, rows), f32))
    pl.semaphore_wait(barrier, R + C - 2)
    for h in range(H):
        u_buf[h] = jnp.zeros((n, rows), f32)
        give_total(h, 0, total[half(h)])
    give_primal(0, [jnp.sum(x_old[h, me] ** 2, axis=1, keepdims=True) for h in range(H)])

    order = list(range(1, chips)) + [0]

    def iteration(step, carry):
        now = lax.rem(step, 2)
        sends = []

        def send(c):
            c.start()
            sends.append(c)

        def backward(both_dual, high, q):
            both = matmul(both_dual, k_hi[q], False)
            return both[:n] + both[n:] + matmul(high, k_lo[q], False)

        duals, dual_parts = [], []
        for h in range(H):
            dual, moved = dual_half(h, 1 - now)
            high, low = split(dual)
            both_dual = jnp.concatenate([high, low], axis=0)
            duals.append((both_dual, high))
            dual_parts.append(moved)
            for o in order:
                p = chip_at(o)
                a_src[h, o] = backward(both_dual, high, 2 * p + 1 - core)
                send(copy(a_src.at[h, o], a_dst.at[h, p], a_sem, (h, o), "rows", sibling))
        give_norms(1 - now, dual_parts)
        images = []
        for h in range(H):
            for o in order:
                p = chip_at(o)
                mine = backward(*duals[h], 2 * p + core)
                copy(a_src.at[h, o], a_dst.at[h, p], a_sem, (h, o), "rows", sibling).wait_recv()
                mine = mine + a_dst[h, p]
                if o > 0:
                    b_src[h, o] = mine
                    send(copy(b_src.at[h, o], b_dst.at[h, o], b_sem, (h, o), "rows", 2 * p + core))
            images.append(mine)
        take_norms()
        at = columns(me)
        primal_parts, fields = [], []
        for h in range(H):
            image = images[h]
            for o in range(1, chips):
                copy(b_src.at[h, o], b_dst.at[h, o], b_sem, (h, o), "rows", 2 * chip_at(o) + core).wait_recv()
                image = image + b_dst[h, o]
            tau = (steps[half(h)] / weights[half(h)])[:, :1]
            before = x_old[h, me]
            fresh = project(before - tau * (obj_ref[:, at] - image), at)
            block = x_new.at[h, me]
            block[...] = fresh
            for o in range(1, chips):
                send(copy(block, block, c_sem, (h, o), "rows", 2 * chip_at(o) + core))
            send(copy(block, block, c_sem, (h, 0), "rows", sibling))
            primal_parts.append(jnp.sum((fresh - before) ** 2, axis=1, keepdims=True))
            fields.append(2.0 * fresh - before)
            x_old[h, me] = fresh
        give_primal(now, primal_parts)
        totals = [forward(fields[h], me) for h in range(H)]

        def add(h, q):
            fresh = x_new[h, q]
            field = 2.0 * fresh - x_old[h, q]
            x_old[h, q] = fresh
            totals[h] = totals[h] + forward(field, q)

        for h in range(H):
            block = x_new.at[h, sibling]
            copy(block, block, c_sem, (h, 0), "rows", sibling).wait_recv()
            add(h, sibling)
        for h in range(H):
            for o in range(1, chips):
                q = 2 * chip_from(o) + core
                block = x_new.at[h, q]
                copy(block, block, c_sem, (h, o), "rows", 2 * chip_at(o) + core).wait_recv()
                send(copy(block, block, f_sem, (h, o), "rows", sibling))
                add(h, q)
        for h in range(H):
            for o in range(1, chips):
                q = 2 * chip_from(o) + 1 - core
                block = x_new.at[h, q]
                copy(block, block, f_sem, (h, o), "rows", sibling).wait_recv()
                add(h, q)
            give_total(h, now, totals[h])
        for c in sends:
            c.wait_send()
        return carry

    lax.fori_loop(1, ITERS, iteration, 0)
    stores = []
    for h in range(H):
        for q in range(R):
            c = pltpu.make_async_copy(x_old.at[h, q], x_hbm.at[half(h), q * chunk : (q + 1) * chunk], out_sem.at[h, q])
            c.start()
            stores.append(c)
    last = (ITERS - 1) % 2
    dual_parts = []
    for h in range(H):
        dual_parts.append(dual_half(h, last)[1])
    give_norms(last, dual_parts)
    for h in range(H):
        c = pltpu.make_async_copy(u_buf.at[h], u_hbm.at[half(h)], out_sem.at[h, R])
        c.start()
        stores.append(c)
    take_norms()
    final = jnp.broadcast_to(weights[:, :1], (S, S))
    w_ref[...] = jnp.sum(jnp.where(eye, final, 0.0), axis=0, keepdims=True)
    for c in stores:
        c.wait()


def hand_out(x_from, u_from, w_from, x_to, u_to, w_to, x_mid, u_mid, w_mid, sem):
    trips = ((x_from, x_mid, x_to), (u_from, u_mid, u_to), (w_from, w_mid, w_to))
    loads = [pltpu.make_async_copy(a, b, sem.at[0, i]) for i, (a, b, _) in enumerate(trips)]
    stores = [pltpu.make_async_copy(b, c, sem.at[1, i]) for i, (_, b, c) in enumerate(trips)]
    for c in loads:
        c.start()
    for load, store in zip(loads, stores):
        load.wait()
        store.start()
    for c in stores:
        c.wait()


def solution(mesh):
    R, C = mesh.shape["rows"], mesh.shape["cols"]

    def local(blocks, ell_index, counts, objective, lower, upper, var_kind, demand, row_kind, step_size, primal_weight):
        row_blocks, _, slots, width, _ = blocks.shape
        n_vars = objective.shape[0]
        S, rows = demand.shape
        H = HALVES
        n, chunk, chips = S // H, n_vars // R, R // 2
        hbm = pl.BlockSpec(memory_space=pltpu.HBM)
        primal, dual, weight = pl.pallas_call(
            functools.partial(kernel, R, C),
            out_shape=(
                jax.ShapeDtypeStruct((S, n_vars), f32),
                jax.ShapeDtypeStruct((S, rows), f32),
                jax.ShapeDtypeStruct((1, S), f32),
            ),
            in_specs=[hbm] * 11,
            out_specs=(hbm, hbm, pl.BlockSpec(memory_space=pltpu.VMEM)),
            scratch_shapes=[
                pltpu.VMEM((row_blocks, slots, width, width), f32),
                pltpu.VMEM(ell_index.shape, jnp.int32),
                pltpu.VMEM((1, row_blocks), jnp.int32),
                pltpu.VMEM((1, n_vars), f32),
                pltpu.VMEM((1, n_vars), f32),
                pltpu.VMEM((1, n_vars), f32),
                pltpu.VMEM((1, n_vars), jnp.int32),
                pltpu.VMEM((S, rows), f32),
                pltpu.VMEM((1, rows), jnp.int32),
                pltpu.VMEM((1, S), f32),
                pltpu.VMEM((1, S), f32),
                pltpu.VMEM((row_blocks, LANES), jnp.int32),
                pltpu.SMEM((row_blocks, LANES), jnp.int32),
                pltpu.VMEM((R, rows, chunk), bf16),
                pltpu.VMEM((R, rows, chunk), bf16),
                pltpu.VMEM((H, chips, n, chunk), f32),
                pltpu.VMEM((H, chips, n, chunk), f32),
                pltpu.VMEM((H, chips, n, chunk), f32),
                pltpu.VMEM((H, chips, n, chunk), f32),
                pltpu.VMEM((H, R, n, chunk), f32),
                pltpu.VMEM((H, R, n, chunk), f32),
                pltpu.VMEM((2, H, C, n, rows), f32),
                pltpu.VMEM((H, n, rows), f32),
                pltpu.VMEM((2, C, SUB, LANES), f32),
                pltpu.VMEM((R, SUB, LANES), f32),
                pltpu.VMEM((S, LANES), f32),
                pltpu.VMEM((S, LANES), f32),
                pltpu.SemaphoreType.DMA((12,)),
                pltpu.SemaphoreType.DMA((H, R + 1)),
                pltpu.SemaphoreType.DMA((2, H, chips)),
                pltpu.SemaphoreType.DMA((2, H, chips)),
                pltpu.SemaphoreType.DMA((2, H, chips)),
                pltpu.SemaphoreType.DMA((2, H, chips)),
                pltpu.SemaphoreType.DMA((2, 2, H, C)),
                pltpu.SemaphoreType.DMA((2, 2, C)),
                pltpu.SemaphoreType.DMA((2, R)),
            ],
            compiler_params=pltpu.CompilerParams(
                collective_id=0, has_side_effects=True, vmem_limit_bytes=64 * 1024 * 1024
            ),
        )(
            blocks,
            ell_index,
            counts.reshape(1, row_blocks),
            objective.reshape(1, n_vars),
            lower.reshape(1, n_vars),
            upper.reshape(1, n_vars),
            var_kind.reshape(1, n_vars),
            demand,
            row_kind.reshape(1, rows),
            step_size.reshape(1, S),
            primal_weight.reshape(1, S),
        )
        primal, dual, weight = pl.pallas_call(
            hand_out,
            out_shape=tuple(jax.ShapeDtypeStruct(a.shape, f32) for a in (primal, dual, weight)),
            in_specs=[hbm] * 3,
            out_specs=(hbm,) * 3,
            scratch_shapes=[
                pltpu.VMEM(primal.shape, f32),
                pltpu.VMEM(dual.shape, f32),
                pltpu.VMEM(weight.shape, f32),
                pltpu.SemaphoreType.DMA((2, 3)),
            ],
            compiler_params=pltpu.CompilerParams(vmem_limit_bytes=64 * 1024 * 1024),
        )(primal, dual, weight)
        return primal, dual, weight.reshape(S)

    return jax.shard_map(
        local,
        mesh=mesh,
        in_specs=(
            P("rows", "cols", None, None, None),
            P("rows", "cols", None),
            P("rows", "cols"),
            P("cols"),
            P("cols"),
            P("cols"),
            P("cols"),
            P(None, "rows"),
            P("rows"),
            P(),
            P(),
        ),
        out_specs=(P(None, "cols"), P(None, "rows"), P()),
        check_vma=False,
    )
```
